32 devices in a mesh: seq: 8 (over z, y), head: 4 (over x, core).
Axes of the slice: x: 2, y: 2, z: 4, core: 2. Of those that a mesh axis runs over, the one named last changes fastest.
Arguments:
- hidden: bfloat16 [1024, 1024], P('seq', 'head'), may hold values from -6 to 6
- queries: bfloat16 [1024, 1024], P('seq', 'head'), may hold values from -40 to 40
- suffix_keys: bfloat16 [1024, 1024], P('seq', 'head'), may hold values from -4 to 4
- suffix_values: bfloat16 [1024, 1024], P('seq', 'head'), may hold values from -6 to 6
- lengths: int32 [8], P('seq'), may hold values from 1 to 128, 640 in all
- key_cache: bfloat16 [8, 32, 1024], P('seq', None, 'head'), may hold values from -6 to 6
- value_cache: bfloat16 [8, 32, 1024], P('seq', None, 'head'), may hold values from -6 to 6
- page_group: int32 [8], replicated, may hold values from 0 to 3, as said below
- out_weight: bfloat16 [1024, 1024], P('head'), may hold values from -0.1875 to 0.1875
- norm_gain: float32 [1024], replicated, may hold values from 0.1 to 1.9
- router_weight: bfloat16 [1024, 16], P('head'), may hold values from -0.1875 to 0.1875
- routes: int32 [1024, 2], P('seq'), may hold values from 0 to 15, all different within a row; in each aligned block of 128 rows (0 to 127, 128 to 255, ...) at most 20 rows name the same one
- gate_weight: bfloat16 [16, 1024, 2816], P('seq', None, 'head'), as said below
- up_weight: bfloat16 [16, 1024, 2816], P('seq', None, 'head'), as said below
- down_weight: bfloat16 [16, 1024, 2816], P('seq', None, 'head'), as said below
- destinations: int32 [8], replicated, may hold values from 0 to 7, as said below
Outputs:
- layer_output: bfloat16 [1024, 1024], P('seq', 'head')
The draws below stay inside these ranges and needn't reach their ends.
Inputs may be any that keep to these rules, and one draw needn't show every extreme that they name: `lengths`: the largest length is 128. `page_group`: each of the 4 groups is named by exactly 2 entries. `routes`: each row names 2 different experts; in each aligned block of 128 rows no expert is named by more than 20 rows. `gate_weight`: copies h and h2 with h == h2 // 1 are equal. `up_weight`: copies h and h2 with h == h2 // 1 are equal. `down_weight`: copies h and h2 with h == h2 // 1 are equal. `destinations`: A permutation of the requests in which exactly 2 requests change place.
All inputs are finite; a program needn't handle non-finite values. No bound on the sum of `lengths` on one device may be relied on, other than what follows from the above.
Results may differ from the reference program's by a relative error of at most 0.0065.
Values may be sent and summed in bfloat16 or wider, within the bound.
A program may use at most 64 MiB of HBM per device.

```python
import math
import jax
import jax.numpy as jnp
import numpy as np
from jax import lax

D = 1024
HEADS = 16
DH = 64
EXPERTS = 16
FF = 2816
TOPK = 2
ROWS = 128
PAGE = 32
GROUPS = 4
REQS = 8
TOKENS = 1024
PAGES = 8
GROUP_PAGES = 2
PREFIX = 64
REPLICAS = 1
HOSTS = 16
SUB_ROWS = 128
CAP = 20
MIGRATE = 2


def attention_pair(key):
    key_queries, key_keys = jax.random.split(jax.random.fold_in(key, 11), 2)
    array_shape = (TOKENS, HEADS * DH)
    base_queries = jnp.clip(jax.random.normal(key_queries, array_shape, jnp.float32), -4.0, 4.0)
    base_keys = jnp.clip(jax.random.normal(key_keys, array_shape, jnp.float32), -4.0, 4.0)
    return (base_queries, base_keys)


def draw_queries(key, part):
    return attention_pair(key)[0].astype(jnp.bfloat16)


def draw_suffix_keys(key, part):
    return attention_pair(key)[1].astype(jnp.bfloat16)


def draw_page_group(key, part):
    shuffled = jax.random.permutation(jax.random.fold_in(key, 5), PAGES).astype(jnp.int32)
    return (shuffled // GROUP_PAGES).astype(jnp.int32)


def draw_destinations(key, part):
    shuffled = jax.random.permutation(jax.random.fold_in(key, 3), REQS).astype(jnp.int32)
    movers = shuffled[:MIGRATE]
    targets = jnp.roll(movers, 1)
    return jnp.arange(REQS, dtype=jnp.int32).at[movers].set(targets)


def placed_experts(key, salt, fan_in):
    base_key = jax.random.fold_in(key, salt)

    def one_copy(copy_index):
        expert_key = jax.random.fold_in(base_key, copy_index // REPLICAS)
        values = jax.random.normal(expert_key, (D, FF), jnp.float32)
        return jnp.clip(values, -6.0, 6.0) * fan_in ** (-0.5)
    return jax.lax.map(one_copy, jnp.arange(HOSTS, dtype=jnp.int32))


def draw_gate_weight(key, part):
    return placed_experts(key, 21, D).astype(jnp.bfloat16)


def draw_up_weight(key, part):
    return placed_experts(key, 22, D).astype(jnp.bfloat16)


def draw_down_weight(key, part):
    return placed_experts(key, 23, FF).astype(jnp.bfloat16)


def steps_of(rng, dims, pieces, smallest, high):
    level, own = 1.0, jax.random.fold_in(rng, 6)
    for dim, shards_of in pieces:
        heights = jnp.exp(jax.random.uniform(jax.random.fold_in(own, dim), (shards_of,), jnp.float32, smallest / len(pieces), high / len(pieces)))
        level = level * jnp.repeat(heights, dims[dim] // shards_of).reshape([-1 if axis == dim else 1 for axis in range(len(dims))])
    return level


def split_up(amount, total, reach, lean):
    weights = [(1 << 20) // math.isqrt(rank ** lean) + 1 for rank in range(2, amount + 1)]
    rest, given = total - reach - (amount - 1), [1] * (amount - 1)
    while rest > 0:
        free = [i for i in range(amount - 1) if given[i] < reach]
        whole, budget = sum([weights[i] for i in free]), rest
        for i in free:
            extra = min(reach - given[i], max(1, budget * weights[i] // whole), rest)
            given[i] = given[i] + extra
            rest = rest - extra
    return np.array([reach] + given)


def uneven(stream_key, count, total, reach, slope):
    if count == 2:
        one = jax.random.randint(stream_key, (), max(1, total - reach), min(reach, total - 1) + 1)
        return jnp.stack([one, total - one])
    sizes = jnp.asarray(split_up(count, total, reach, slope), jnp.int32)
    couples = (count - 1) // 2
    giver, taker = sizes[1:1 + 2 * couples:2], sizes[2:2 + 2 * couples:2]
    slack = jnp.minimum(giver - 1, reach - taker)
    shifted = jax.random.randint(jax.random.fold_in(stream_key, 1), (couples,), 0, 1 << 20) % (slack + 1)
    sizes = sizes.at[1:1 + 2 * couples:2].set(giver - shifted).at[2:2 + 2 * couples:2].set(taker + shifted)
    return sizes[jax.random.permutation(jax.random.fold_in(stream_key, 2), count)]


def shared_out(own_key, own, number, rows, amount, top, most, slope):
    sequence = jax.random.permutation(own_key, amount)
    crowded, ordinary = portions_of(amount, rows * top, most, slope, True), portions_of(amount, rows * top, most, slope, False)
    places = jnp.arange(amount)

    def named(sizes, rotation):
        used = int((sizes > 0).sum())
        fixed = max(1, used // 4)
        passed = fixed + (places - fixed + rotation * (used - fixed)) % max(1, amount - fixed)
        return jnp.zeros((amount,), jnp.int32).at[sequence[jnp.where(places < fixed, places, passed)]].set(jnp.asarray(sizes, jnp.int32))

    sizes = jnp.where(number % 4 == 0, named(crowded, number // 4), named(ordinary, number - number // 4 - 1))
    mixed = jax.random.permutation(jax.random.fold_in(own, 3), amount)
    giver, receiver = mixed[0:amount // 2 * 2:2], mixed[1:amount // 2 * 2:2]
    margin = jnp.minimum(sizes[giver] - 1, most - sizes[receiver]) // 2
    margin = jnp.where((giver == sequence[0]) | (receiver == sequence[0]) | (sizes[receiver] == 0), 0, jnp.maximum(margin, 0))
    passed = jax.random.randint(jax.random.fold_in(own, 4), (amount // 2,), 0, 1 << 20) % (margin + 1)
    sizes = sizes.at[giver].add(-passed).at[receiver].add(passed)
    labels = jnp.searchsorted(jnp.cumsum(sizes), jnp.arange(rows * top), side="right").astype(jnp.int32)
    grid = labels.reshape(top, rows).T
    grid = grid[jax.random.permutation(jax.random.fold_in(own, 1), rows)]
    rotation = jax.random.randint(jax.random.fold_in(own, 2), (rows, 1), 0, top)
    return jnp.take_along_axis(grid, (jnp.arange(top)[None, :] + rotation) % top, axis=1)


def portions_of(amount, total, reach, skew, full):
    portions = [(1 << 20) // math.isqrt(grade ** skew) + 1 for grade in range(1, amount + 1)]
    largest = reach if full else min(reach, max(-(-total // amount), total * portions[0] // sum(portions)))
    least = 1 if total - largest >= amount - 1 else 0
    given, spare = [largest] + [least] * (amount - 1), total - largest - least * (amount - 1)
    while spare > 0:
        movable = [i for i in range(1, amount) if given[i] < largest] or [i for i in range(1, amount) if given[i] < reach]
        whole, budget = sum([portions[i] for i in movable]), spare
        for i in movable:
            extra = min(reach - given[i], max(1, budget * portions[i] // whole), spare)
            given[i] = given[i] + extra
            spare = spare - extra
    return np.array(given)


def normal_values(rng, extent, scale, limit, shards=(), held_as=jnp.bfloat16):
    level = steps_of(rng, extent, shards, -0.22, 0.18) if shards else 1.0
    entries = jax.random.normal(rng, extent, jnp.float32) * scale * level
    return jnp.minimum(jnp.maximum(entries, -limit), limit).astype(held_as)


def setup_inputs(seed: int = 0) -> dict:
    streams_of = jax.random.split(jax.random.key(seed), 17)
    hidden = normal_values(streams_of[0], (TOKENS, D), 1.0, 6.0, ((0, 8), (1, 4)))
    queries = draw_queries(jax.random.fold_in(streams_of[16], 71), 0)
    suffix_keys = draw_suffix_keys(jax.random.fold_in(streams_of[16], 71), 0)
    suffix_values = normal_values(streams_of[3], (TOKENS, HEADS * DH), 1.0, 6.0, ((0, 8), (1, 4)))
    lengths = uneven(streams_of[4], REQS, REQS * ROWS * 5 // 8, ROWS, 1).astype(jnp.int32)
    key_cache = normal_values(streams_of[5], (PAGES, PAGE, HEADS * DH), 1.0, 6.0, ((0, 8), (2, 4)))
    value_cache = normal_values(streams_of[6], (PAGES, PAGE, HEADS * DH), 1.0, 6.0, ((0, 8), (2, 4)))
    page_group = draw_page_group(jax.random.fold_in(streams_of[16], 71), 0)
    out_weight = normal_values(streams_of[8], (HEADS * DH, D), (HEADS * DH) ** -0.5, 0.1875, ((0, 4),))
    norm_gain = jnp.clip(1.0 + 0.18 * jax.random.normal(streams_of[9], (D,), jnp.float32), 0.1, 1.9)
    router_weight = normal_values(streams_of[10], (D, EXPERTS), D ** -0.5, 0.1875, ((0, 4),))
    routes_keys = jax.random.split(jax.random.fold_in(streams_of[11], 1), TOKENS // SUB_ROWS)
    routes_turns = jax.random.permutation(jax.random.fold_in(streams_of[11], 3), TOKENS // SUB_ROWS)
    routes = jax.vmap(lambda own, number: shared_out(jax.random.fold_in(streams_of[11], 2), own, number, SUB_ROWS, EXPERTS, TOPK, CAP, 2))(routes_keys, routes_turns).reshape((TOKENS, TOPK))
    gate_weight = draw_gate_weight(jax.random.fold_in(streams_of[16], 71), 0)
    up_weight = draw_up_weight(jax.random.fold_in(streams_of[16], 71), 0)
    down_weight = draw_down_weight(jax.random.fold_in(streams_of[16], 71), 0)
    destinations = draw_destinations(jax.random.fold_in(streams_of[16], 71), 0)
    return {"hidden": hidden, "queries": queries, "suffix_keys": suffix_keys, "suffix_values": suffix_values, "lengths": lengths, "key_cache": key_cache, "value_cache": value_cache, "page_group": page_group, "out_weight": out_weight, "norm_gain": norm_gain, "router_weight": router_weight, "routes": routes, "gate_weight": gate_weight, "up_weight": up_weight, "down_weight": down_weight, "destinations": destinations}


norm_eps = 1e-06

def page_inverse(page_group, group_pages, groups):
    page_total = page_group.shape[0]
    onehot = (page_group[:, None] == jnp.arange(groups, dtype=jnp.int32)[None, :]).astype(jnp.int32)
    page_rank = lax.optimization_barrier(jnp.sum((jnp.cumsum(onehot, axis=0) - 1) * onehot, axis=1))
    target = page_group * group_pages + page_rank
    return jnp.zeros((page_total,), jnp.int32).at[target].set(jnp.arange(page_total, dtype=jnp.int32))

def attend_request(query_rows, key_rows, value_rows, prefix_keys, prefix_values, length, head_total):
    row_count = query_rows.shape[0]
    head_size = query_rows.shape[1] // head_total
    scale = head_size ** (-0.5)

    def heads_of(array):
        return array.reshape(array.shape[0], head_total, head_size).astype(jnp.float32)
    prefix_scores = jnp.einsum('qhd,khd->hqk', heads_of(query_rows), heads_of(prefix_keys)) * scale
    suffix_scores = jnp.einsum('qhd,khd->hqk', heads_of(query_rows), heads_of(key_rows)) * scale
    query_pos = jnp.arange(row_count, dtype=jnp.int32)[:, None]
    key_pos = jnp.arange(row_count, dtype=jnp.int32)[None, :]
    allowed = (key_pos <= query_pos) & (key_pos < length)
    suffix_scores = jnp.where(allowed[None], suffix_scores, -jnp.inf)
    row_max = jnp.maximum(lax.optimization_barrier(jnp.max(prefix_scores, axis=2)), lax.optimization_barrier(jnp.max(suffix_scores, axis=2)))[..., None]
    prefix_exp = jnp.exp(prefix_scores - row_max)
    suffix_exp = jnp.exp(suffix_scores - row_max)
    denominators = lax.optimization_barrier(jnp.sum(prefix_exp, axis=2, keepdims=True)) + lax.optimization_barrier(jnp.sum(suffix_exp, axis=2, keepdims=True))
    prefix_probs = (prefix_exp / denominators).astype(jnp.bfloat16)
    suffix_probs = (suffix_exp / denominators).astype(jnp.bfloat16)
    mixed_heads = jnp.einsum('hqk,khd->qhd', prefix_probs.astype(jnp.float32), heads_of(prefix_values))
    mixed_heads = mixed_heads + jnp.einsum('hqk,khd->qhd', suffix_probs.astype(jnp.float32), heads_of(value_rows))
    return mixed_heads.reshape(row_count, head_total * head_size).astype(jnp.bfloat16)

def reference(hidden, queries, suffix_keys, suffix_values, lengths, key_cache, value_cache, page_group, out_weight, norm_gain, router_weight, routes, gate_weight, up_weight, down_weight, destinations):
    inverse = page_inverse(page_group, GROUP_PAGES, GROUPS)
    block_requests = REQS // GROUPS
    features = HEADS * DH

    def one_request(request):
        start = (request * ROWS).astype(jnp.int32)
        query_rows = lax.dynamic_slice_in_dim(queries, start, ROWS, 0)
        key_rows = lax.dynamic_slice_in_dim(suffix_keys, start, ROWS, 0)
        value_rows = lax.dynamic_slice_in_dim(suffix_values, start, ROWS, 0)
        group_index = (request // block_requests).astype(jnp.int32)
        page_index = lax.dynamic_slice_in_dim(inverse, group_index * GROUP_PAGES, GROUP_PAGES, 0)
        prefix_keys = jnp.take(key_cache, page_index, axis=0).reshape(PREFIX, features)
        prefix_values = jnp.take(value_cache, page_index, axis=0).reshape(PREFIX, features)
        return attend_request(query_rows, key_rows, value_rows, prefix_keys, prefix_values, lengths[request], HEADS)
    attended = lax.map(one_request, jnp.arange(REQS, dtype=jnp.int32)).reshape(TOKENS, features)
    resid = hidden.astype(jnp.float32) + jnp.dot(attended, out_weight, preferred_element_type=jnp.float32)
    normed = (resid * lax.rsqrt(lax.optimization_barrier(jnp.mean(resid * resid, axis=1, keepdims=True)) + norm_eps) * norm_gain).astype(jnp.bfloat16)
    logits = jnp.dot(normed, router_weight, preferred_element_type=jnp.float32)
    chosen = jnp.take_along_axis(logits, routes, axis=1)
    gate_first = jax.nn.sigmoid(chosen[:, 0] - chosen[:, 1])
    gate_second = jax.nn.sigmoid(chosen[:, 1] - chosen[:, 0])
    pair_total = TOKENS * TOPK
    expert_ids = routes.reshape(-1)
    order = jnp.argsort(expert_ids, stable=True).astype(jnp.int32)
    counts = lax.optimization_barrier(jnp.sum((expert_ids[:, None] == jnp.arange(EXPERTS, dtype=jnp.int32)[None, :]).astype(jnp.int32), axis=0))
    starts = (jnp.cumsum(counts) - counts).astype(jnp.int32)
    most_rows = REQS * REPLICAS * CAP
    padded_order = jnp.concatenate([order, jnp.zeros((most_rows,), jnp.int32)])

    def one_expert(expert):
        pair_index = lax.dynamic_slice_in_dim(padded_order, starts[expert], most_rows, 0)
        valid = jnp.arange(most_rows, dtype=jnp.int32) < counts[expert]
        token_rows = jnp.take(normed, pair_index // TOPK, axis=0)
        copy_index = expert * REPLICAS
        gate_act = jnp.dot(token_rows, gate_weight[copy_index], preferred_element_type=jnp.float32)
        up_act = jnp.dot(token_rows, up_weight[copy_index], preferred_element_type=jnp.float32)
        expert_hidden = (jax.nn.gelu(gate_act, approximate=True) * up_act).astype(jnp.bfloat16)
        expert_out = jnp.dot(expert_hidden, down_weight[copy_index].T, preferred_element_type=jnp.float32).astype(jnp.bfloat16)
        return (jnp.where(valid[:, None], expert_out, jnp.zeros_like(expert_out)), pair_index)
    outputs, pair_indices = lax.map(one_expert, jnp.arange(EXPERTS, dtype=jnp.int32))
    pair_out = jnp.zeros((pair_total, D), jnp.float32).at[pair_indices.reshape(-1)].add(outputs.reshape(-1, D).astype(jnp.float32))
    pair_out = pair_out.reshape(TOKENS, TOPK, D)
    layer = resid + gate_first[:, None] * pair_out[:, 0] + gate_second[:, None] * pair_out[:, 1]
    layer = layer.astype(jnp.bfloat16)
    positions = jnp.arange(ROWS, dtype=jnp.int32)
    live_rows = (positions[None, :] < lengths[:, None]).reshape(TOKENS)
    layer = jnp.where(live_rows[:, None], layer, jnp.zeros_like(layer))
    by_request = layer.reshape(REQS, ROWS, D)
    placed = jnp.zeros_like(by_request).at[destinations].set(by_request)
    return placed.reshape(TOKENS, D)
```

```python
import functools

import jax
import jax.numpy as jnp
from jax import lax
from jax.experimental import pallas as pl
from jax.experimental.pallas import tpu as pltpu
from jax.sharding import PartitionSpec as P

DH = 64
EXPERTS = 16
TOPK = 2
GROUPS = 4
norm_eps = 1e-06

F32, BF16, I32 = jnp.float32, jnp.bfloat16, jnp.int32
NT = (((1,), (1,)), ((), ()))
TN = (((0,), (0,)), ((), ()))


def mm(a, b, dims=(((1,), (0,)), ((), ()))):
    return lax.dot_general(a, b, dims, preferred_element_type=F32)


def iota(shape, dim):
    return lax.broadcasted_iota(I32, shape, dim)


def remote(src, dst, send, recv, **where):
    return pltpu.make_async_remote_copy(
        src_ref=src,
        dst_ref=dst,
        send_sem=send,
        recv_sem=recv,
        device_id=where,
        device_id_type=pl.DeviceIdType.MESH,
    )


def each(low, high, step):
    if high - low <= 16:
        for i in range(low, high):
            step(i)
        return

    def body(i, carry):
        step(i)
        return carry

    lax.fori_loop(low, high, body, 0)


def layer_kernel(
    cfg,
    lengths,
    page_group,
    destinations,
    hidden,
    queries,
    keys,
    values,
    key_cache,
    value_cache,
    out_weight,
    gain,
    router,
    routes,
    gate_hbm,
    up_hbm,
    down_hbm,
    out,
    gate_w,
    up_w,
    down_w,
    key_pages,
    value_pages,
    ow,
    att,
    squares,
    diffs,
    send_rows,
    slots,
    partial,
    pair_send,
    pair_recv,
    cross_send,
    cross_recv,
    home_send,
    returned,
    piece_send,
    pieces,
    place_send,
    placed,
    weight_sem,
    page_sem,
    head_sem,
    seq_sem,
    fwd_sem,
    back_sem,
):
    S, H, per_device, replicas, capacity, pair_rows, inside = cfg
    me, h = lax.axis_index("seq"), lax.axis_index("head")
    rows, cols = hidden.shape
    page_local, page_rows, _ = key_cache.shape
    slot_rows = S * pair_rows
    pair = h + 1 - 2 * (h % 2)
    cross = (h + 2) % 4

    loads = [
        pltpu.make_async_copy(a, b, weight_sem.at[i])
        for i, (a, b) in enumerate(((gate_hbm, gate_w), (up_hbm, up_w), (down_hbm, down_w)))
    ]
    for load in loads:
        load.start()

    barrier = pltpu.get_barrier_semaphore()
    each(
        1,
        S,
        lambda i: pl.semaphore_signal(
            barrier, inc=1, device_id={"seq": (me + i) % S}, device_id_type=pl.DeviceIdType.MESH
        ),
    )
    for j in range(1, H):
        pl.semaphore_signal(
            barrier, inc=1, device_id={"head": (h + j) % H}, device_id_type=pl.DeviceIdType.MESH
        )
    pl.semaphore_wait(barrier, S - 1 + H - 1)

    def page_copy(i, which):
        src, dst = ((key_cache, key_pages), (value_cache, value_pages))[which]
        return remote(
            src,
            dst.at[pl.ds(me * page_local, page_local)],
            page_sem.at[which, 0, i],
            page_sem.at[which, 1, i],
            seq=(me + i) % S,
        )

    def start_pages(i):
        page_copy(i, 0).start()
        page_copy(i, 1).start()

    each(1, S, start_pages)
    key_pages[pl.ds(me * page_local, page_local)] = key_cache[...]
    value_pages[pl.ds(me * page_local, page_local)] = value_cache[...]

    def head_copy(kind, j):
        to = (h + j) % H
        src, dst = (
            (out_weight.at[:, pl.ds(pl.multiple_of(to * cols, cols), cols)], ow.at[h]),
            (att.at[h], att.at[h]),
            (squares.at[h], squares.at[h]),
            (diffs.at[h], diffs.at[h]),
        )[kind]
        return remote(src, dst, head_sem.at[kind, 0, j], head_sem.at[kind, 1, j], head=to)

    for j in range(1, H):
        head_copy(0, j).start()
    ow[h] = out_weight[:, pl.ds(pl.multiple_of(h * cols, cols), cols)]

    eye = iota((rows, rows), 0) == iota((rows, rows), 1)

    def as_row(column):
        row = jnp.sum(jnp.where(eye, column, 0.0), axis=0, keepdims=True)
        return jnp.broadcast_to(row, (8, rows))

    def as_column(row):
        return jnp.sum(jnp.where(eye, row, 0.0), axis=1, keepdims=True)

    expert = iota((rows, EXPERTS), 1)
    named = routes[...].astype(F32)
    is_first = (as_column(named[0:1]).astype(I32) == expert).astype(F32)
    is_second = (as_column(named[1:2]).astype(I32) == expert).astype(F32)
    sub_rows = rows // replicas
    before = (iota((rows, rows), 1) < iota((rows, rows), 0)) & (
        iota((rows, rows), 1) // sub_rows == iota((rows, rows), 0) // sub_rows
    )
    rank = mm(before.astype(F32).astype(BF16), (is_first + is_second).astype(BF16))
    target = expert // per_device * replicas + iota((rows, EXPERTS), 0) // sub_rows
    slot = (target * pair_rows + expert % per_device * capacity).astype(F32) + rank
    slot_of = [
        jnp.sum(one * slot, axis=1, keepdims=True).astype(I32) for one in (is_first, is_second)
    ]
    slot_ids = iota((rows, slot_rows), 1)
    choose = [(slot_ids == s).astype(F32).astype(BF16) for s in slot_of]

    heads = cols // DH
    lane_head = iota((rows, cols), 1) // DH
    query = queries[...]
    stacked = jnp.concatenate(
        [jnp.where(lane_head == n, query, jnp.zeros_like(query)) for n in range(heads)], axis=0
    )
    scale = DH ** (-0.5)
    suffix = mm(stacked, keys[...], NT) * scale
    position = iota((heads * rows, rows), 0) % rows
    key_position = iota((heads * rows, rows), 1)
    suffix = jnp.where(
        (key_position <= position) & (key_position < lengths[0]), suffix, -jnp.inf
    )

    group = me // (S // GROUPS)

    lane_page = iota((1, S * page_local * page_rows), 1) // page_rows

    def mark(p, held):
        return jnp.where((lane_page == p) & (page_group[p] == group), 1.0, held)

    ours = lax.fori_loop(0, S * page_local, mark, jnp.zeros(lane_page.shape, F32))

    def wait_pages(i):
        page_copy(i, 0).wait_recv()
        page_copy(i, 1).wait_recv()

    each(1, S, wait_pages)
    prefix_keys = key_pages[...].reshape(-1, cols)
    prefix_values = value_pages[...].reshape(-1, cols)
    prefix = jnp.where(ours > 0.5, mm(stacked, prefix_keys, NT) * scale, -jnp.inf)
    top = jnp.maximum(
        jnp.max(prefix, axis=1, keepdims=True), jnp.max(suffix, axis=1, keepdims=True)
    )
    prefix = jnp.exp(prefix - top)
    suffix = jnp.exp(suffix - top)
    total = jnp.sum(prefix, axis=1, keepdims=True) + jnp.sum(suffix, axis=1, keepdims=True)
    mixed = mm((prefix / total).astype(BF16), prefix_values) + mm(
        (suffix / total).astype(BF16), values[...]
    )
    attended = jnp.zeros((rows, cols), F32)
    for n in range(heads):
        attended = jnp.where(lane_head == n, mixed[n * rows : (n + 1) * rows], attended)
    att[h] = attended.astype(BF16)
    for j in range(1, H):
        head_copy(1, j).start()
    for j in range(1, H):
        head_copy(0, j).wait_recv()
    for j in range(1, H):
        head_copy(1, j).wait_recv()
    resid = hidden[...].astype(F32)
    for j in range(H):
        resid = resid + mm(att[j], ow[j])

    squares[h] = as_row(jnp.sum(resid * resid, axis=1, keepdims=True))
    for j in range(1, H):
        head_copy(2, j).start()
    for j in range(1, H):
        head_copy(2, j).wait_recv()
    square = as_column((squares[0] + squares[1] + squares[2] + squares[3])[0:1])
    normed = (
        resid * lax.rsqrt(square / (H * cols) + norm_eps) * gain[pl.ds(h, 1), :]
    ).astype(BF16)

    send_rows[...] = mm(choose[0] + choose[1], normed, TN).astype(BF16)

    def block(s):
        return pl.ds(pl.multiple_of(s * pair_rows, pair_rows), pair_rows)

    def dispatch(i):
        to = (me + i) % S
        return remote(
            send_rows.at[block(to)],
            slots.at[h, block(me)],
            seq_sem.at[0, 0, i],
            seq_sem.at[0, 1, i],
            seq=to,
        )

    each(1, S, lambda i: dispatch(i).start())
    slots[h, block(me)] = send_rows[block(me)]

    def forward(kind, i):
        source = (me + S - i) % S
        held = slots.at[cross if kind == 2 else h, block(source)]
        return remote(
            held,
            held,
            fwd_sem.at[kind, 0, i],
            fwd_sem.at[kind, 1, i],
            head=cross if kind == 1 else pair,
        )

    forward(1, 0).start()
    forward(0, 0).start()
    logits = mm(normed, router[...], NT)
    diffs[h] = as_row(jnp.sum((is_first - is_second) * logits, axis=1, keepdims=True))
    for j in range(1, H):
        head_copy(3, j).start()

    def pass_on(i):
        dispatch(i).wait_recv()
        forward(1, i).start()
        forward(0, i).start()

    each(1, S, pass_on)

    def pass_across(i):
        forward(1, i).wait_recv()
        forward(2, i).start()

    each(0, S, pass_across)
    for load in loads:
        load.wait()

    def wait_forward(i):
        forward(0, i).wait_recv()
        forward(2, i).wait_recv()

    each(0, S, wait_forward)

    def expert_rows(p, parts):
        gate_act = sum(mm(parts[j], gate_w[p, :, j * cols : (j + 1) * cols], NT) for j in range(H))
        up_act = sum(mm(parts[j], up_w[p, :, j * cols : (j + 1) * cols], NT) for j in range(H))
        inner = 0.7978845608028654 * (gate_act + 0.044715 * gate_act * gate_act * gate_act)
        act = (0.5 * gate_act * (1.0 + jnp.tanh(inner)) * up_act).astype(BF16)
        return [mm(act, down_w[p, :, j * cols : (j + 1) * cols]) for j in range(H)]

    if per_device == 1:
        chunk = min(256, slot_rows)

        def one_chunk(i):
            at = pl.ds(pl.multiple_of(i * chunk, chunk), chunk)
            done = expert_rows(0, [slots[j, at] for j in range(H)])
            for j in range(H):
                partial[j, at] = done[j]

        each(0, slot_rows // chunk, one_chunk)
    else:
        own = S * capacity
        row, column = iota((own, slot_rows), 0), iota((own, slot_rows), 1)
        for p in range(per_device):
            pick = (
                (column == row // capacity * pair_rows + p * capacity + row % capacity)
                .astype(F32)
                .astype(BF16)
            )
            done = expert_rows(p, [mm(pick, slots[j]).astype(BF16) for j in range(H)])
            for j in range(H):
                back = mm(pick, done[j].astype(BF16), TN)
                partial[j] = back if p == 0 else partial[j] + back

    pair_send[0] = partial[pair].astype(BF16)
    pair_send[1] = partial[(pair + 2) % 4].astype(BF16)
    pair_copies = [
        remote(
            pair_send.at[n],
            pair_recv.at[n],
            back_sem.at[0, 0, n],
            back_sem.at[0, 1, n],
            head=pair,
        )
        for n in range(2)
    ]
    pair_copies[1].start()
    pair_copies[0].start()
    pair_copies[1].wait_recv()
    cross_send[...] = (partial[cross] + pair_recv[1].astype(F32)).astype(BF16)

    def cross_copy(i):
        at = block((me + i) % S)
        return remote(
            cross_send.at[at],
            cross_recv.at[at],
            back_sem.at[1, 0, i],
            back_sem.at[1, 1, i],
            head=cross,
        )

    each(1, S + 1, lambda i: cross_copy(i).start())
    pair_copies[0].wait_recv()

    def home_copy(i):
        to = (me + i) % S
        return remote(
            home_send.at[block(to)],
            returned.at[block(me)],
            seq_sem.at[1, 0, i],
            seq_sem.at[1, 1, i],
            seq=to,
        )

    def total_block(i):
        at = block((me + i) % S)
        cross_copy(i).wait_recv()
        return (
            partial[h, at] + pair_recv[0, at].astype(F32) + cross_recv[at].astype(F32)
        ).astype(BF16)

    def send_home(i):
        home_send[block((me + i) % S)] = total_block(i)
        home_copy(i).start()

    each(1, S, send_home)
    returned[block(me)] = total_block(S)
    for j in range(1, H):
        head_copy(3, j).wait_recv()
    difference = as_column((diffs[0] + diffs[1] + diffs[2] + diffs[3])[0:1])
    gate_first = 1.0 / (1.0 + jnp.exp(-difference))
    gate_second = 1.0 / (1.0 + jnp.exp(difference))
    each(1, S, lambda i: home_copy(i).wait_recv())
    back = returned[...]
    layer = resid + gate_first * mm(choose[0], back) + gate_second * mm(choose[1], back)
    layer = jnp.where(iota((rows, cols), 0) < lengths[0], layer, 0.0).astype(BF16)

    if not inside:
        out[...] = layer
    else:
        piece = rows // S

        def part(s):
            return pl.ds(pl.multiple_of(s * piece, piece), piece)

        def out_copy(stage, i):
            to = (me + i) % S
            src, dst = ((piece_send, pieces), (place_send, placed))[stage]
            return remote(
                src.at[part(to)],
                dst.at[me] if stage == 0 else dst.at[part(me)],
                seq_sem.at[2 + stage, 0, i],
                seq_sem.at[2 + stage, 1, i],
                seq=to,
            )

        piece_send[...] = layer
        each(1, S, lambda i: out_copy(0, i).start())
        pieces[me] = piece_send[part(me)]
        origin = []
        for d in range(S):
            r = jnp.int32(0)
            for n in range(S):
                r = jnp.where(destinations[n] == d, n, r)
            origin.append(r)
        each(1, S, lambda i: out_copy(0, i).wait_recv())
        for d in range(S):
            taken = jnp.zeros((piece, cols), F32)
            for n in range(S):
                taken = jnp.where(origin[d] == n, pieces[n].astype(F32), taken)
            place_send[d * piece : (d + 1) * piece] = taken.astype(BF16)
        each(1, S, lambda i: out_copy(1, i).start())
        placed[part(me)] = place_send[part(me)]
        each(1, S, lambda i: out_copy(1, i).wait_recv())
        out[...] = placed[...]

    def sent(i):
        page_copy(i, 0).wait_send()
        page_copy(i, 1).wait_send()
        dispatch(i).wait_send()
        home_copy(i).wait_send()
        if inside:
            out_copy(0, i).wait_send()
            out_copy(1, i).wait_send()

    each(1, S, sent)

    def sent_all(i):
        for kind in range(3):
            forward(kind, i).wait_send()
        cross_copy(i + 1).wait_send()

    each(0, S, sent_all)
    for j in range(1, H):
        for kind in range(4):
            head_copy(kind, j).wait_send()
    for n in range(2):
        pair_copies[n].wait_send()


def on_device(
    hidden,
    queries,
    suffix_keys,
    suffix_values,
    lengths,
    key_cache,
    value_cache,
    page_group,
    out_weight,
    norm_gain,
    router_weight,
    routes,
    gate_weight,
    up_weight,
    down_weight,
    destinations,
):
    S, H = lax.axis_size("seq"), lax.axis_size("head")
    rows, cols = hidden.shape
    replicas = max(1, S // EXPERTS)
    per_device = max(1, EXPERTS // S)
    least = 5 * rows * TOPK // (4 * EXPERTS * replicas)
    unit = 16 // min(per_device, 2)
    capacity = -(-least // unit) * unit
    pair_rows = per_device * capacity
    slot_rows = S * pair_rows
    inside = rows % (16 * S) == 0
    pages = S * key_cache.shape[0]
    page_shape = (pages, *key_cache.shape[1:])
    small = rows if inside else 16

    def vmem(*shape, dtype=BF16):
        return pltpu.VMEM(shape, dtype)

    dma = pltpu.SemaphoreType.DMA
    whole = pl.BlockSpec(memory_space=pltpu.VMEM)
    scalars = pl.BlockSpec(memory_space=pltpu.SMEM)
    hbm = pl.BlockSpec(memory_space=pl.ANY)
    gate_weight, up_weight, down_weight = (
        jnp.swapaxes(w, 1, 2) for w in (gate_weight, up_weight, down_weight)
    )
    layer = pl.pallas_call(
        functools.partial(
            layer_kernel, (S, H, per_device, replicas, capacity, pair_rows, inside)
        ),
        out_shape=jax.ShapeDtypeStruct((rows, cols), BF16),
        in_specs=[scalars] * 3 + [whole] * 10 + [hbm] * 3,
        out_specs=whole,
        scratch_shapes=[
            vmem(*gate_weight.shape),
            vmem(*up_weight.shape),
            vmem(*down_weight.shape),
            vmem(*page_shape),
            vmem(*page_shape),
            vmem(H, cols, cols),
            vmem(H, rows, cols),
            vmem(H, 8, rows, dtype=F32),
            vmem(H, 8, rows, dtype=F32),
            vmem(slot_rows, cols),
            vmem(H, slot_rows, cols),
            vmem(H, slot_rows, cols, dtype=F32),
            vmem(2, slot_rows, cols),
            vmem(2, slot_rows, cols),
            vmem(slot_rows, cols),
            vmem(slot_rows, cols),
            vmem(slot_rows, cols),
            vmem(slot_rows, cols),
            vmem(small, cols),
            vmem(S if inside else 1, max(16, rows // S), cols),
            vmem(small, cols),
            vmem(small, cols),
            dma((3,)),
            dma((2, 2, S)),
            dma((4, 2, H)),
            dma((4, 2, S)),
            dma((3, 2, S)),
            dma((2, 2, S + 1)),
        ],
        compiler_params=pltpu.CompilerParams(
            collective_id=0, has_side_effects=True, vmem_limit_bytes=56 * 2**20
        ),
    )(
        lengths,
        page_group,
        destinations,
        hidden,
        queries,
        suffix_keys,
        suffix_values,
        key_cache,
        value_cache,
        out_weight,
        norm_gain.reshape(H, cols),
        router_weight.T,
        routes.T,
        gate_weight,
        up_weight,
        down_weight,
    )
    if inside:
        return layer
    out_pieces = layer.reshape(S, rows // S, cols)
    scattered = lax.all_to_all(out_pieces, "seq", split_axis=0, concat_axis=0, tiled=True)
    index = jnp.arange(S, dtype=I32)
    origin = jnp.sum(jnp.where(destinations[None, :] == index[:, None], index[None, :], 0), axis=1)
    chosen = (origin[:, None] == index[None, :]).astype(BF16)
    reordered = jnp.dot(chosen, scattered.reshape(S, -1), preferred_element_type=F32)
    reordered = reordered.astype(BF16).reshape(scattered.shape)
    settled = lax.all_to_all(reordered, "seq", split_axis=0, concat_axis=0, tiled=True)
    return settled.reshape(rows, cols)


def solution(mesh):
    return jax.shard_map(
        on_device,
        mesh=mesh,
        in_specs=(
            P("seq", "head"),
            P("seq", "head"),
            P("seq", "head"),
            P("seq", "head"),
            P("seq"),
            P("seq", None, "head"),
            P("seq", None, "head"),
            P(),
            P("head", None),
            P(),
            P("head", None),
            P("seq", None),
            P("seq", None, "head"),
            P("seq", None, "head"),
            P("seq", None, "head"),
            P(),
        ),
        out_specs=P("seq", "head"),
        check_vma=False,
    )
```

```python
import functools

import jax
import jax.numpy as jnp
from jax import lax
from jax.experimental import pallas as pl
from jax.experimental.pallas import tpu as pltpu
from jax.sharding import PartitionSpec as P

DH = 64
EXPERTS = 16
TOPK = 2
GROUPS = 4
norm_eps = 1e-06

F32, BF16, I32 = jnp.float32, jnp.bfloat16, jnp.int32
NT = (((1,), (1,)), ((), ()))
TN = (((0,), (0,)), ((), ()))


def mm(a, b, dims=(((1,), (0,)), ((), ()))):
    return lax.dot_general(a, b, dims, preferred_element_type=F32)


def iota(shape, dim):
    return lax.broadcasted_iota(I32, shape, dim)


def remote(src, dst, send, recv, **where):
    return pltpu.make_async_remote_copy(
        src_ref=src,
        dst_ref=dst,
        send_sem=send,
        recv_sem=recv,
        device_id=where,
        device_id_type=pl.DeviceIdType.MESH,
    )


def each(low, high, step):
    if high - low <= 16:
        for i in range(low, high):
            step(i)
        return

    def body(i, carry):
        step(i)
        return carry

    lax.fori_loop(low, high, body, 0)


def layer_kernel(
    cfg,
    lengths,
    page_group,
    destinations,
    hidden,
    queries,
    keys,
    values,
    key_cache,
    value_cache,
    out_weight,
    gain,
    router,
    routes,
    gate_hbm,
    up_hbm,
    down_hbm,
    out,
    gate_w,
    up_w,
    down_w,
    key_pages,
    value_pages,
    ow,
    att,
    squares,
    diffs,
    send_rows,
    slots,
    partial,
    pair_send,
    pair_recv,
    cross_send,
    cross_recv,
    home_send,
    returned,
    piece_send,
    pieces,
    place_send,
    placed,
    weight_sem,
    page_sem,
    head_sem,
    seq_sem,
    fwd_sem,
    back_sem,
):
    S, H, per_device, replicas, capacity, pair_rows, inside = cfg
    me, h = lax.axis_index("seq"), lax.axis_index("head")
    rows, cols = hidden.shape
    page_local, page_rows, _ = key_cache.shape
    slot_rows = S * pair_rows
    pair = h + 1 - 2 * (h % 2)
    cross = (h + 2) % 4

    loads = [
        pltpu.make_async_copy(a, b, weight_sem.at[i])
        for i, (a, b) in enumerate(((gate_hbm, gate_w), (up_hbm, up_w), (down_hbm, down_w)))
    ]
    for load in loads:
        load.start()

    barrier = pltpu.get_barrier_semaphore()
    each(
        1,
        S,
        lambda i: pl.semaphore_signal(
            barrier, inc=1, device_id={"seq": (me + i) % S}, device_id_type=pl.DeviceIdType.MESH
        ),
    )
    for j in range(1, H):
        pl.semaphore_signal(
            barrier, inc=1, device_id={"head": (h + j) % H}, device_id_type=pl.DeviceIdType.MESH
        )
    pl.semaphore_wait(barrier, S - 1 + H - 1)

    def columns(b):
        return pl.ds(pl.multiple_of(b * cols, cols), cols)

    def page_copy(i, which):
        src, dst = ((key_cache, key_pages), (value_cache, value_pages))[which]
        return remote(
            src,
            dst.at[pl.ds(me * page_local, page_local)],
            page_sem.at[which, 0, i],
            page_sem.at[which, 1, i],
            seq=(me + i) % S,
        )

    def start_pages(i):
        page_copy(i, 0).start()
        page_copy(i, 1).start()

    each(1, S, start_pages)
    key_pages[pl.ds(me * page_local, page_local)] = key_cache[...]
    value_pages[pl.ds(me * page_local, page_local)] = value_cache[...]

    def head_copy(kind, j):
        to = (h + j) % H
        src, dst = (
            (out_weight.at[:, pl.ds(pl.multiple_of(to * cols, cols), cols)], ow.at[h]),
            (att.at[h], att.at[h]),
            (squares.at[h], squares.at[h]),
            (diffs.at[h], diffs.at[h]),
        )[kind]
        return remote(src, dst, head_sem.at[kind, 0, j], head_sem.at[kind, 1, j], head=to)

    for j in range(1, H):
        head_copy(0, j).start()
    ow[h] = out_weight[:, pl.ds(pl.multiple_of(h * cols, cols), cols)]

    eye = iota((rows, rows), 0) == iota((rows, rows), 1)

    def as_row(column):
        row = jnp.sum(jnp.where(eye, column, 0.0), axis=0, keepdims=True)
        return jnp.broadcast_to(row, (8, rows))

    def as_column(row):
        return jnp.sum(jnp.where(eye, row, 0.0), axis=1, keepdims=True)

    expert = iota((rows, EXPERTS), 1)
    named = routes[...].astype(F32)
    is_first = (as_column(named[0:1]).astype(I32) == expert).astype(F32)
    is_second = (as_column(named[1:2]).astype(I32) == expert).astype(F32)
    sub_rows = rows // replicas
    before = (iota((rows, rows), 1) < iota((rows, rows), 0)) & (
        iota((rows, rows), 1) // sub_rows == iota((rows, rows), 0) // sub_rows
    )
    rank = mm(before.astype(F32).astype(BF16), (is_first + is_second).astype(BF16))
    target = expert // per_device * replicas + iota((rows, EXPERTS), 0) // sub_rows
    slot = (target * pair_rows + expert % per_device * capacity).astype(F32) + rank
    slot_of = [
        jnp.sum(one * slot, axis=1, keepdims=True).astype(I32) for one in (is_first, is_second)
    ]
    slot_ids = iota((rows, slot_rows), 1)
    choose = [(slot_ids == s).astype(F32).astype(BF16) for s in slot_of]

    heads = cols // DH
    lane_head = iota((rows, cols), 1) // DH
    query = queries[...]
    stacked = jnp.concatenate(
        [jnp.where(lane_head == n, query, jnp.zeros_like(query)) for n in range(heads)], axis=0
    )
    scale = DH ** (-0.5)
    suffix = mm(stacked, keys[...], NT) * scale
    position = iota((heads * rows, rows), 0) % rows
    key_position = iota((heads * rows, rows), 1)
    suffix = jnp.where(
        (key_position <= position) & (key_position < lengths[0]), suffix, -jnp.inf
    )

    group = me // (S // GROUPS)

    lane_page = iota((1, S * page_local * page_rows), 1) // page_rows

    def mark(p, held):
        return jnp.where((lane_page == p) & (page_group[p] == group), 1.0, held)

    ours = lax.fori_loop(0, S * page_local, mark, jnp.zeros(lane_page.shape, F32))

    def wait_pages(i):
        page_copy(i, 0).wait_recv()
        page_copy(i, 1).wait_recv()

    each(1, S, wait_pages)
    prefix_keys = key_pages[...].reshape(-1, cols)
    prefix_values = value_pages[...].reshape(-1, cols)
    prefix = jnp.where(ours > 0.5, mm(stacked, prefix_keys, NT) * scale, -jnp.inf)
    top = jnp.maximum(
        jnp.max(prefix, axis=1, keepdims=True), jnp.max(suffix, axis=1, keepdims=True)
    )
    prefix = jnp.exp(prefix - top)
    suffix = jnp.exp(suffix - top)
    total = jnp.sum(prefix, axis=1, keepdims=True) + jnp.sum(suffix, axis=1, keepdims=True)
    mixed = mm((prefix / total).astype(BF16), prefix_values) + mm(
        (suffix / total).astype(BF16), values[...]
    )
    attended = jnp.zeros((rows, cols), F32)
    for n in range(heads):
        attended = jnp.where(lane_head == n, mixed[n * rows : (n + 1) * rows], attended)
    att[h] = attended.astype(BF16)
    for j in range(1, H):
        head_copy(1, j).start()
    for j in range(1, H):
        head_copy(0, j).wait_recv()
    for j in range(1, H):
        head_copy(1, j).wait_recv()
    resid = hidden[...].astype(F32)
    for j in range(H):
        resid = resid + mm(att[j], ow[j])

    squares[h] = as_row(jnp.sum(resid * resid, axis=1, keepdims=True))
    for j in range(1, H):
        head_copy(2, j).start()
    for j in range(1, H):
        head_copy(2, j).wait_recv()
    square = as_column((squares[0] + squares[1] + squares[2] + squares[3])[0:1])
    normed = (
        resid * lax.rsqrt(square / (H * cols) + norm_eps) * gain[:, columns(h)]
    ).astype(BF16)

    send_rows[...] = mm(choose[0] + choose[1], normed, TN).astype(BF16)

    def block(s):
        return pl.ds(pl.multiple_of(s * pair_rows, pair_rows), pair_rows)

    def dispatch(i):
        to = (me + i) % S
        return remote(
            send_rows.at[block(to)],
            slots.at[h, block(me)],
            seq_sem.at[0, 0, i],
            seq_sem.at[0, 1, i],
            seq=to,
        )

    each(1, S, lambda i: dispatch(i).start())
    slots[h, block(me)] = send_rows[block(me)]

    def forward(kind, i):
        source = (me + S - i) % S
        held = slots.at[cross if kind == 2 else h, block(source)]
        return remote(
            held,
            held,
            fwd_sem.at[kind, 0, i],
            fwd_sem.at[kind, 1, i],
            head=cross if kind == 1 else pair,
        )

    forward(1, 0).start()
    forward(0, 0).start()
    logits = mm(normed, router[...], NT)
    diffs[h] = as_row(jnp.sum((is_first - is_second) * logits, axis=1, keepdims=True))
    for j in range(1, H):
        head_copy(3, j).start()

    def pass_on(i):
        dispatch(i).wait_recv()
        forward(1, i).start()
        forward(0, i).start()

    for load in loads:
        load.wait()
    each(1, S, pass_on)

    def pass_across(i):
        forward(1, i).wait_recv()
        forward(2, i).start()

    def activate(gate_act, up_act):
        inner = 0.7978845608028654 * (gate_act + 0.044715 * gate_act * gate_act * gate_act)
        return (0.5 * gate_act * (1.0 + jnp.tanh(inner)) * up_act).astype(BF16)

    last = (pair + 2) % 4
    if per_device == 1:
        each(0, S, pass_across)
        each(0, S, lambda i: forward(0, i).wait_recv())
        each(0, S, lambda i: forward(2, i).wait_recv())
        chunk = min(256, slot_rows)

        def one_chunk(i):
            at = pl.ds(pl.multiple_of(i * chunk, chunk), chunk)
            gate_act, up_act = (
                sum(mm(slots[j, at], w[0, :, j * cols : (j + 1) * cols], NT) for j in range(H))
                for w in (gate_w, up_w)
            )
            act = activate(gate_act, up_act)
            for j in range(H):
                partial[j, at] = mm(act, down_w[0, :, j * cols : (j + 1) * cols])

        each(0, slot_rows // chunk, one_chunk)

        def block_out(b):
            return partial[b]

    else:
        own = S * capacity
        row, column = iota((own, slot_rows), 0), iota((own, slot_rows), 1)
        picks = [
            (column == row // capacity * pair_rows + p * capacity + row % capacity)
            .astype(F32)
            .astype(BF16)
            for p in range(per_device)
        ]
        sums = [None] * per_device

        def feed(b):
            for p in range(per_device):
                x = mm(picks[p], slots[b]).astype(BF16)
                more = [mm(x, w[p, :, columns(b)], NT) for w in (gate_w, up_w)]
                sums[p] = more if sums[p] is None else [m + n for m, n in zip(sums[p], more)]

        feed(h)
        each(0, S, pass_across)
        each(0, S, lambda i: forward(0, i).wait_recv())
        feed(pair)
        feed(cross)
        each(0, S, lambda i: forward(2, i).wait_recv())
        feed(last)
        acts = [activate(*sums[p]) for p in range(per_device)]

        def block_out(b):
            return sum(
                mm(picks[p], mm(acts[p], down_w[p, :, columns(b)]).astype(BF16), TN)
                for p in range(per_device)
            )

    pair_copies = [
        remote(
            pair_send.at[n],
            pair_recv.at[n],
            back_sem.at[0, 0, n],
            back_sem.at[0, 1, n],
            head=pair,
        )
        for n in range(2)
    ]
    pair_send[1] = block_out(last).astype(BF16)
    pair_copies[1].start()
    crossing = block_out(cross)
    pair_copies[1].wait_recv()
    cross_send[...] = (crossing + pair_recv[1].astype(F32)).astype(BF16)

    def cross_copy(i):
        at = block((me + i) % S)
        return remote(
            cross_send.at[at],
            cross_recv.at[at],
            back_sem.at[1, 0, i],
            back_sem.at[1, 1, i],
            head=cross,
        )

    each(1, S + 1, lambda i: cross_copy(i).start())
    pair_send[0] = block_out(pair).astype(BF16)
    pair_copies[0].start()
    partial[h] = block_out(h)
    pair_copies[0].wait_recv()

    def home_copy(i):
        to = (me + i) % S
        return remote(
            home_send.at[block(to)],
            returned.at[block(me)],
            seq_sem.at[1, 0, i],
            seq_sem.at[1, 1, i],
            seq=to,
        )

    def total_block(i):
        at = block((me + i) % S)
        cross_copy(i).wait_recv()
        return (
            partial[h, at] + pair_recv[0, at].astype(F32) + cross_recv[at].astype(F32)
        ).astype(BF16)

    def send_home(i):
        home_send[block((me + i) % S)] = total_block(i)
        home_copy(i).start()

    each(1, S, send_home)
    returned[block(me)] = total_block(S)
    for j in range(1, H):
        head_copy(3, j).wait_recv()
    difference = as_column((diffs[0] + diffs[1] + diffs[2] + diffs[3])[0:1])
    gate_first = 1.0 / (1.0 + jnp.exp(-difference))
    gate_second = 1.0 / (1.0 + jnp.exp(difference))
    each(1, S, lambda i: home_copy(i).wait_recv())
    back = returned[...]
    layer = resid + gate_first * mm(choose[0], back) + gate_second * mm(choose[1], back)
    layer = jnp.where(iota((rows, cols), 0) < lengths[0], layer, 0.0).astype(BF16)

    if not inside:
        out[...] = layer
    else:
        piece = rows // S

        def part(s):
            return pl.ds(pl.multiple_of(s * piece, piece), piece)

        def out_copy(stage, i):
            to = (me + i) % S
            src, dst = ((piece_send, pieces), (place_send, placed))[stage]
            return remote(
                src.at[part(to)],
                dst.at[me] if stage == 0 else dst.at[part(me)],
                seq_sem.at[2 + stage, 0, i],
                seq_sem.at[2 + stage, 1, i],
                seq=to,
            )

        piece_send[...] = layer
        each(1, S, lambda i: out_copy(0, i).start())
        pieces[me] = piece_send[part(me)]
        origin = []
        for d in range(S):
            r = jnp.int32(0)
            for n in range(S):
                r = jnp.where(destinations[n] == d, n, r)
            origin.append(r)
        each(1, S, lambda i: out_copy(0, i).wait_recv())
        for d in range(S):
            taken = jnp.zeros((piece, cols), F32)
            for n in range(S):
                taken = jnp.where(origin[d] == n, pieces[n].astype(F32), taken)
            place_send[d * piece : (d + 1) * piece] = taken.astype(BF16)
        each(1, S, lambda i: out_copy(1, i).start())
        placed[part(me)] = place_send[part(me)]
        each(1, S, lambda i: out_copy(1, i).wait_recv())
        out[...] = placed[...]

    def sent(i):
        page_copy(i, 0).wait_send()
        page_copy(i, 1).wait_send()
        dispatch(i).wait_send()
        home_copy(i).wait_send()
        if inside:
            out_copy(0, i).wait_send()
            out_copy(1, i).wait_send()

    each(1, S, sent)

    def sent_all(i):
        for kind in range(3):
            forward(kind, i).wait_send()
        cross_copy(i + 1).wait_send()

    each(0, S, sent_all)
    for j in range(1, H):
        for kind in range(4):
            head_copy(kind, j).wait_send()
    for n in range(2):
        pair_copies[n].wait_send()


def on_device(
    hidden,
    queries,
    suffix_keys,
    suffix_values,
    lengths,
    key_cache,
    value_cache,
    page_group,
    out_weight,
    norm_gain,
    router_weight,
    routes,
    gate_weight,
    up_weight,
    down_weight,
    destinations,
):
    S, H = lax.axis_size("seq"), lax.axis_size("head")
    rows, cols = hidden.shape
    replicas = max(1, S // EXPERTS)
    per_device = max(1, EXPERTS // S)
    least = 5 * rows * TOPK // (4 * EXPERTS * replicas)
    unit = 16 // min(per_device, 2)
    capacity = -(-least // unit) * unit
    pair_rows = per_device * capacity
    slot_rows = S * pair_rows
    inside = rows % (16 * S) == 0
    pages = S * key_cache.shape[0]
    page_shape = (pages, *key_cache.shape[1:])
    small = rows if inside else 16

    def vmem(*shape, dtype=BF16):
        return pltpu.VMEM(shape, dtype)

    dma = pltpu.SemaphoreType.DMA
    whole = pl.BlockSpec(memory_space=pltpu.VMEM)
    scalars = pl.BlockSpec(memory_space=pltpu.SMEM)
    hbm = pl.BlockSpec(memory_space=pl.ANY)
    gate_weight, up_weight, down_weight = (
        jnp.swapaxes(w, 1, 2) for w in (gate_weight, up_weight, down_weight)
    )
    layer = pl.pallas_call(
        functools.partial(
            layer_kernel, (S, H, per_device, replicas, capacity, pair_rows, inside)
        ),
        out_shape=jax.ShapeDtypeStruct((rows, cols), BF16),
        in_specs=[scalars] * 3 + [whole] * 10 + [hbm] * 3,
        out_specs=whole,
        scratch_shapes=[
            vmem(*gate_weight.shape),
            vmem(*up_weight.shape),
            vmem(*down_weight.shape),
            vmem(*page_shape),
            vmem(*page_shape),
            vmem(H, cols, cols),
            vmem(H, rows, cols),
            vmem(H, 8, rows, dtype=F32),
            vmem(H, 8, rows, dtype=F32),
            vmem(slot_rows, cols),
            vmem(H, slot_rows, cols),
            vmem(H, slot_rows, cols, dtype=F32),
            vmem(2, slot_rows, cols),
            vmem(2, slot_rows, cols),
            vmem(slot_rows, cols),
            vmem(slot_rows, cols),
            vmem(slot_rows, cols),
            vmem(slot_rows, cols),
            vmem(small, cols),
            vmem(S if inside else 1, max(16, rows // S), cols),
            vmem(small, cols),
            vmem(small, cols),
            dma((3,)),
            dma((2, 2, S)),
            dma((4, 2, H)),
            dma((4, 2, S)),
            dma((3, 2, S)),
            dma((2, 2, S + 1)),
        ],
        compiler_params=pltpu.CompilerParams(
            collective_id=0, has_side_effects=True, vmem_limit_bytes=56 * 2**20
        ),
    )(
        lengths,
        page_group,
        destinations,
        hidden,
        queries,
        suffix_keys,
        suffix_values,
        key_cache,
        value_cache,
        out_weight,
        norm_gain.reshape(1, H * cols),
        router_weight.T,
        routes.T,
        gate_weight,
        up_weight,
        down_weight,
    )
    if inside:
        return layer
    out_pieces = layer.reshape(S, rows // S, cols)
    scattered = lax.all_to_all(out_pieces, "seq", split_axis=0, concat_axis=0, tiled=True)
    index = jnp.arange(S, dtype=I32)
    origin = jnp.sum(jnp.where(destinations[None, :] == index[:, None], index[None, :], 0), axis=1)
    chosen = (origin[:, None] == index[None, :]).astype(BF16)
    reordered = jnp.dot(chosen, scattered.reshape(S, -1), preferred_element_type=F32)
    reordered = reordered.astype(BF16).reshape(scattered.shape)
    settled = lax.all_to_all(reordered, "seq", split_axis=0, concat_axis=0, tiled=True)
    return settled.reshape(rows, cols)


def solution(mesh):
    return jax.shard_map(
        on_device,
        mesh=mesh,
        in_specs=(
            P("seq", "head"),
            P("seq", "head"),
            P("seq", "head"),
            P("seq", "head"),
            P("seq"),
            P("seq", None, "head"),
            P("seq", None, "head"),
            P(),
            P("head", None),
            P(),
            P("head", None),
            P("seq", None),
            P("seq", None, "head"),
            P("seq", None, "head"),
            P("seq", None, "head"),
            P(),
        ),
        out_specs=P("seq", "head"),
        check_vma=False,
    )
```
